32 devices in a mesh: groups: 2 (over x), clu: 16 (over z, y, core).
Axes of the slice: x: 2, y: 2, z: 4, core: 2. Of those that a mesh axis runs over, the one named last changes fastest.
Arguments:
- charges: bfloat16 [64, 65536], P(None, ('groups', 'clu')), parts along dimension 1, may hold values from -6 to 6
- coords: bfloat16 [3, 65536], P(None, ('groups', 'clu')), parts along dimension 1, may hold values from -1 to 1
- requests: int32 [32, 16, 2], P(('groups', 'clu')), parts along dimension 0, may hold values from 0 to 7
- near_rows: int32 [32, 128], P(('groups', 'clu')), parts along dimension 0, may hold values from 0 to 7, as said below
- near_src: int32 [32, 128], P(('groups', 'clu')), parts along dimension 0, may hold values from 0 to 15, as said below
- local_pairs: int32 [32, 2, 16], P(('groups', 'clu')), parts along dimension 0, may hold values from 0 to 7, as said below
- far_rows: int32 [32, 256], P(('groups', 'clu')), parts along dimension 0, may hold values from 0 to 7, as said below
- far_slots: int32 [32, 256], P(('groups', 'clu')), parts along dimension 0, may hold values from 0 to 31
- far_left: bfloat16 [8192, 32, 256], P(('groups', 'clu')), parts along dimension 0, may hold values from -0.5 to 0.5
- far_right: bfloat16 [8192, 32, 256], P(('groups', 'clu')), parts along dimension 0, may hold values from -0.375 to 0.375
Outputs:
- potential: float32 [64, 65536], P(None, ('groups', 'clu')), parts along dimension 1
The draws below stay inside these ranges and needn't reach their ends.
There are 2 independent parts, one for each index of `groups`. The reference program is written for one: setup_inputs(seed, part) draws one part's arguments, and reference() takes and returns one part's arrays. A program takes and returns all parts, laid end to end along the dimension named above; each array names one. Nothing has to cross between parts.
Inputs may be any that keep to these rules, and one draw needn't show every extreme that they name: requests[d, p, s] is the local index of a cluster of device p; device d reads that cluster into slot p * 2 + s. Within a device no pair (near_rows, near_src) repeats. near_src[d, k] = w names cluster 8 * (d + 1) + w, a cluster of one of the next two devices; indices past the last cluster mark unused pairs. local_pairs[d, 0, k] < local_pairs[d, 1, k], and no pair repeats within a device. Within a device no pair (far_rows, far_slots) repeats.
All inputs are finite; a program needn't handle non-finite values.
Results may differ from the reference program's by a relative error of at most 0.0029.
Values may be sent and summed in bfloat16 or wider, within the bound.
A program may use at most 128 MiB of HBM per device.

```python
import jax
import jax.numpy as jnp
import numpy as np
from jax import lax

CL_SIZE = 256
RHS = 64
RANK = 32
SLOTS = 2
CL_DEV = 8
NEAR_LOC = 16
NEAR_REM = 128
FAR_DEV = 256
READS = 32
CLUSTERS = 128
PANELS = 32768
FAR_TOTAL = 4096
N_CLU = 16


def near_draw(key):
    device_keys = jax.random.split(jax.random.fold_in(key, 21), N_CLU)
    width = 2 * CL_DEV

    def one_device(device_key):
        chosen = jax.random.permutation(device_key, CL_DEV * width)[:NEAR_REM]
        return ((chosen // width).astype(jnp.int32), (chosen % width).astype(jnp.int32))
    return jax.vmap(one_device)(device_keys)


def far_draw(key):
    device_keys = jax.random.split(jax.random.fold_in(key, 31), N_CLU)

    def one_device(device_key):
        chosen = jax.random.permutation(device_key, CL_DEV * READS)[:FAR_DEV]
        return ((chosen // READS).astype(jnp.int32), (chosen % READS).astype(jnp.int32))
    return jax.vmap(one_device)(device_keys)


def draw_near_rows(key, part):
    return near_draw(key)[0]


def draw_near_src(key, part):
    return near_draw(key)[1]


def draw_far_rows(key, part):
    return far_draw(key)[0]


def draw_far_slots(key, part):
    return far_draw(key)[1]


def draw_local_pairs(key, part):
    key = jax.random.fold_in(key, 11)
    upper_first, upper_second = np.triu_indices(CL_DEV, 1)
    special = CL_DEV - 2
    others = np.array([index for index in range(len(upper_first)) if index != special], dtype=np.int32)
    first_table = jnp.asarray(upper_first.astype(np.int32))
    second_table = jnp.asarray(upper_second.astype(np.int32))
    other_table = jnp.asarray(others)
    device_keys = jax.random.split(key, N_CLU)

    def one_device(device_key):
        order = jax.random.permutation(device_key, others.shape[0])
        chosen = jnp.concatenate([jnp.array([special], jnp.int32), other_table[order]])[:NEAR_LOC]
        return jnp.stack([first_table[chosen], second_table[chosen]], axis=0)
    return jax.vmap(one_device)(device_keys)


def place_ends(entries, stream_key, smallest, top_value):
    spot = [jax.random.randint(jax.random.fold_in(stream_key, axis), (), 0, length) for axis, length in enumerate(entries.shape)]
    main_axis = entries.shape.index(max(entries.shape))
    beside = spot[:main_axis] + [(spot[main_axis] + 1) % entries.shape[main_axis]] + spot[main_axis + 1:]
    return entries.at[tuple(spot)].set(smallest).at[tuple(beside)].set(top_value)


def levels(stream_key, shape, cuts, smallest, high):
    factor_of, own = 1.0, jax.random.fold_in(stream_key, 6)
    for axis_at, blocks in cuts:
        draws = jnp.exp(jax.random.uniform(jax.random.fold_in(own, axis_at), (blocks,), jnp.float32, smallest / len(cuts), high / len(cuts)))
        factor_of = factor_of * jnp.repeat(draws, shape[axis_at] // blocks).reshape([-1 if axis == axis_at else 1 for axis in range(len(shape))])
    return factor_of


def gaussian(stream_key, dims, scale, reach, shards=(), held_as=jnp.bfloat16):
    values = jax.random.normal(stream_key, dims, jnp.float32) * scale
    if len(shards) > 0:
        values = levels(stream_key, dims, shards, -0.22, 0.18) * values
    return jnp.clip(values, min=-reach, max=reach).astype(held_as)


def setup_inputs(seed: int = 0, part: int = 0) -> dict:
    key_list = jax.random.split(jax.random.key(seed), 11)
    own_keys = jax.random.split(jax.random.fold_in(key_list[10], part), 11)
    charges = gaussian(own_keys[0], (RHS, PANELS), 1.0, 6.0, ((1, 16),))
    coords = jnp.clip(jax.random.uniform(own_keys[1], (3, PANELS), jnp.float32, -1.0, 1.0) * levels(own_keys[1], (3, PANELS), ((1, 16),), -0.4, 0.0), -1.0, 1.0).astype(jnp.bfloat16)
    requests = place_ends(jax.random.randint(own_keys[2], (N_CLU, N_CLU, SLOTS), 0, CL_DEV), jax.random.fold_in(own_keys[2], 1), 0, CL_DEV - 1).astype(jnp.int32)
    near_rows = draw_near_rows(jax.random.fold_in(jax.random.fold_in(key_list[10], part), 71), part)
    near_src = draw_near_src(jax.random.fold_in(jax.random.fold_in(key_list[10], part), 71), part)
    local_pairs = draw_local_pairs(jax.random.fold_in(jax.random.fold_in(key_list[10], part), 71), part)
    far_rows = draw_far_rows(jax.random.fold_in(jax.random.fold_in(key_list[10], part), 71), part)
    far_slots = draw_far_slots(jax.random.fold_in(jax.random.fold_in(key_list[10], part), 71), part)
    far_left = gaussian(own_keys[8], (FAR_TOTAL, RANK, CL_SIZE), (4 * RANK) ** -0.5, 0.5, ((0, 16),))
    far_right = gaussian(own_keys[9], (FAR_TOTAL, RANK, CL_SIZE), CL_SIZE ** -0.5, 0.375, ((0, 16),))
    return {"charges": charges, "coords": coords, "requests": requests, "near_rows": near_rows, "near_src": near_src, "local_pairs": local_pairs, "far_rows": far_rows, "far_slots": far_slots, "far_left": far_left, "far_right": far_right}


kernel_scale = 1.0 / 64.0
softening = 0.04

def kernel_block(row_points, source_points):
    row_values = row_points.astype(jnp.float32)
    source_values = source_points.astype(jnp.float32)
    squared = (row_values[:, 0, :, None] - source_values[:, 0, None, :]) ** 2
    squared = squared + (row_values[:, 1, :, None] - source_values[:, 1, None, :]) ** 2
    squared = squared + (row_values[:, 2, :, None] - source_values[:, 2, None, :]) ** 2
    return (kernel_scale / jnp.sqrt(squared + softening)).astype(jnp.bfloat16)

def widen(values):
    return lax.optimization_barrier(values).astype(jnp.float32)

def reference(charges, coords, requests, near_rows, near_src, local_pairs, far_rows, far_slots, far_left, far_right):
    charge_blocks = charges.reshape(RHS, CLUSTERS, CL_SIZE).transpose(1, 0, 2)
    charge_wide = charge_blocks.astype(jnp.float32)
    coord_blocks = coords.reshape(3, CLUSTERS, CL_SIZE).transpose(1, 0, 2)
    slot_owner = jnp.arange(READS, dtype=jnp.int32) // SLOTS * CL_DEV
    left_dev = far_left.reshape(N_CLU, FAR_DEV, RANK, CL_SIZE)
    right_dev = far_right.reshape(N_CLU, FAR_DEV, RANK, CL_SIZE)

    def device_step(potential, inputs):
        device, asked_row, target_row, window_row, pair_row, far_row_ids, far_slot_ids, left_here, right_here = inputs
        first_cluster = device * CL_DEV
        sources = slot_owner + asked_row.reshape(-1).astype(jnp.int32)
        targets = (first_cluster + target_row).astype(jnp.int32)
        raw_source = (first_cluster + CL_DEV + window_row).astype(jnp.int32)
        valid = (raw_source < CLUSTERS).astype(jnp.float32)[:, None, None]
        picked = jnp.minimum(raw_source, CLUSTERS - 1).astype(jnp.int32)
        kernel = widen(kernel_block(coord_blocks[targets], coord_blocks[picked]))
        near_term = jnp.einsum('pab,pnb->pna', kernel, charge_wide[picked]) * valid
        back_term = jnp.einsum('pab,pna->pnb', kernel, charge_wide[targets]) * valid
        potential = potential.at[targets].add(near_term).at[picked].add(back_term)
        firsts = (first_cluster + pair_row[0]).astype(jnp.int32)
        seconds = (first_cluster + pair_row[1]).astype(jnp.int32)
        kernel = widen(kernel_block(coord_blocks[firsts], coord_blocks[seconds]))
        potential = potential.at[firsts].add(jnp.einsum('pab,pnb->pna', kernel, charge_wide[seconds]))
        potential = potential.at[seconds].add(jnp.einsum('pab,pna->pnb', kernel, charge_wide[firsts]))
        far_sources = sources[far_slot_ids]
        coefficients = widen(jnp.einsum('pnb,pkb->pnk', charge_wide[far_sources], right_here.astype(jnp.float32)).astype(jnp.bfloat16))
        far_term = jnp.einsum('pnk,pka->pna', coefficients, left_here.astype(jnp.float32))
        potential = potential.at[(first_cluster + far_row_ids).astype(jnp.int32)].add(far_term)
        return (potential, None)
    devices = jnp.arange(N_CLU, dtype=jnp.int32)
    potential = jnp.zeros((CLUSTERS, RHS, CL_SIZE), jnp.float32)
    potential, _ = lax.scan(device_step, potential, (devices, requests, near_rows, near_src, local_pairs, far_rows, far_slots, left_dev, right_dev))
    return potential.transpose(1, 0, 2).reshape(RHS, PANELS)
```

```python
import functools

import jax
import jax.numpy as jnp
from jax import lax
from jax.experimental import pallas as pl
from jax.experimental.pallas import tpu as pltpu
from jax.sharding import PartitionSpec as P

kernel_scale = 1.0 / 64.0
softening = 0.04
MESH = pl.DeviceIdType.MESH
FEATURES = 16
WINDOW = (-2, -1, 1, 2)


def split3(values):
    high = values.astype(jnp.bfloat16)
    rest = values - high.astype(jnp.float32)
    mid = rest.astype(jnp.bfloat16)
    low = (rest - mid.astype(jnp.float32)).astype(jnp.bfloat16)
    return high.astype(jnp.float32), mid.astype(jnp.float32), low.astype(jnp.float32)


def point_features(coords):
    wide = coords.astype(jnp.float32)
    factor = 1.0 / (kernel_scale * kernel_scale)
    norm = (jnp.sum(wide * wide, axis=0, keepdims=True) + 0.5 * softening) * factor
    norms = jnp.concatenate(split3(norm), axis=0)
    ones = jnp.ones_like(norms)
    zeros = jnp.zeros((FEATURES - 9, wide.shape[1]), jnp.float32)
    source = jnp.concatenate([wide, norms, ones, zeros], axis=0)
    target = jnp.concatenate([wide * (-2.0 * factor), ones, norms, zeros], axis=0)
    return source, target


def body(
    n, dense,
    inv_ref, req_ref, q_ref, x_ref, mask_ref, left_hbm, right_hbm,
    out_ref,
    qbuf, fown, fbuf, ft, gown, qgroup, left_v, right_v,
    send_sem, recv_sem, fsend_sem, frecv_sem, load_sem,
):
    columns, width = q_ref.shape
    size = left_hbm.shape[2]
    rank = left_hbm.shape[1]
    clusters = width // size
    zs = n // 4
    me = lax.axis_index("clu")
    z = me // 4
    y = (me // 2) % 2
    core = me % 2
    sib = me + 1 - 2 * core
    other_y = me + 2 - 4 * y

    def block_id(z_at, y_at, core_at):
        return z_at * 4 + y_at * 2 + core_at

    barrier = pltpu.get_barrier_semaphore()
    partners = [(z > 0, me - 4), (z < zs - 1, me + 4), (None, other_y), (None, sib)]
    partners += [((me + off >= 0) & (me + off < n), me + off) for off in WINDOW]
    for valid, partner in partners:
        def greet(partner=partner):
            pl.semaphore_signal(barrier, inc=1, device_id={"clu": partner}, device_id_type=MESH)
        greet() if valid is None else pl.when(valid)(greet)

    if dense:
        load_left = pltpu.make_async_copy(left_hbm, left_v, load_sem.at[0])
        load_right = pltpu.make_async_copy(right_hbm, right_v, load_sem.at[1])
        load_right.start()
        load_left.start()
    source, target = point_features(x_ref[...])
    fown[...] = source.astype(jnp.bfloat16)
    gown[...] = target.astype(jnp.bfloat16)
    for c in range(clusters):
        qbuf[me, c] = q_ref[:, c * size:(c + 1) * size]

    pl.semaphore_wait(
        barrier, sum(1 if valid is None else valid.astype(jnp.int32) for valid, _ in partners)
    )

    sent = []

    def copy_of(block, way, partner):
        return pltpu.make_async_remote_copy(
            src_ref=qbuf.at[block], dst_ref=qbuf.at[block],
            send_sem=send_sem.at[way, block], recv_sem=recv_sem.at[block],
            device_id={"clu": partner}, device_id_type=MESH,
        )

    def send(block, way, partner, valid=None):
        def go():
            copy_of(block, way, partner).start()
        go() if valid is None else pl.when(valid)(go)
        sent.append((block, way, partner, valid))

    def arrive(block, valid=None):
        def go():
            copy_of(block, 0, sib).wait_recv()
        go() if valid is None else pl.when(valid)(go)

    def feature_copy(index):
        off = WINDOW[index]
        return pltpu.make_async_remote_copy(
            src_ref=fown, dst_ref=fbuf.at[index],
            send_sem=fsend_sem.at[index], recv_sem=frecv_sem.at[index],
            device_id={"clu": me + off}, device_id_type=MESH,
        )

    def reaches(off):
        return (me + off >= 0) & (me + off < n)

    for index in (1, 2, 0, 3):
        pl.when(reaches(WINDOW[index]))(lambda index=index: feature_copy(index).start())
    send(me, 3, sib)
    send(me, 2, other_y)
    send(me, 0, me + 4, z < zs - 1)
    send(me, 1, me - 4, z > 0)

    def boundary(k):
        if k <= zs - 1:
            for step, way, partner, more in ((-k, 0, me + 4, z < zs - 1), (k, 1, me - 4, z > 0)):
                there = (z + step >= 0) & (z + step < zs)
                block = block_id(z + step, y, core)
                arrive(block, there)
                send(block, way, partner, there & more)
                send(block, 2, other_y, there)
                send(block, 3, sib, there)
        if k <= zs:
            for step in ((0,) if k == 1 else (-(k - 1), k - 1)):
                there = None if step == 0 else (z + step >= 0) & (z + step < zs)
                block = block_id(z + step, 1 - y, core)
                arrive(block, there)
                send(block, 3, sib, there)
        if k == 1:
            arrive(sib)
        else:
            if k - 1 <= zs - 1:
                for step in (-(k - 1), k - 1):
                    arrive(block_id(z + step, y, 1 - core), (z + step >= 0) & (z + step < zs))
            for step in ((0,) if k == 2 else (-(k - 2), k - 2)):
                there = None if step == 0 else (z + step >= 0) & (z + step < zs)
                arrive(block_id(z + step, 1 - y, 1 - core), there)

    def tile(rows, c):
        squared = jnp.dot(
            rows, gown[:, c * size:(c + 1) * size], preferred_element_type=jnp.float32
        )
        return lax.rsqrt(squared).astype(jnp.bfloat16)

    def set_features(values):
        ft[...] = values.astype(jnp.float32).T.astype(jnp.bfloat16)

    out_ref[...] = jnp.zeros_like(out_ref)

    set_features(fown[...])

    def local_step(step, carry):
        for c in range(clusters):
            e = lax.rem(step + 1 + c, clusters)
            at = pl.ds(pl.multiple_of(e * size, size), size)
            charge = qbuf[me, e] * mask_ref[pl.ds(c, 1), at]
            out_ref[:, c * size:(c + 1) * size] += jnp.dot(
                charge, tile(ft[at, :], c), preferred_element_type=jnp.float32
            )
        return carry

    lax.fori_loop(0, clusters - 1, local_step, 0)

    def near(off):
        there = reaches(off)

        @pl.when(there)
        def _():
            for index, sent_off in enumerate(WINDOW):
                @pl.when(off == -sent_off)
                def _(index=index):
                    feature_copy(index).wait_recv()
                    set_features(fbuf[index])

            def near_step(e, carry):
                at = pl.ds(pl.multiple_of(e * size, size), size)
                charge = qbuf[me + off, e]
                rows = ft[at, :]
                for c in range(clusters):
                    out_ref[:, c * size:(c + 1) * size] += jnp.dot(
                        charge, tile(rows, c), preferred_element_type=jnp.float32
                    )
                return carry

            lax.fori_loop(0, clusters, near_step, 0)

    place = me % 4

    def by_place(values):
        result = values[3]
        for index in (2, 1, 0):
            result = jnp.where(place == index, values[index], result)
        return result

    boundary(1)
    near(by_place((1, -1, 1, -1)))
    boundary(2)
    near(by_place((2, 1, -1, -2)))
    boundary(3)
    near(by_place((-1, 2, -2, 1)))
    boundary(4)
    near(by_place((-2, -2, 2, 2)))
    for k in range(5, zs + 3):
        boundary(k)

    if dense:
        load_right.wait()
        load_left.wait()
        slots_each = req_ref.shape[0] // n
        slots = n * slots_each
        group = size // rank
        row_at = lax.broadcasted_iota(jnp.int32, (columns, size), 1) // rank

        def far_group(g, carry):
            for j in range(group):
                slot = g * group + j
                qgroup[j * columns:(j + 1) * columns, :] = qbuf[slot // slots_each, req_ref[slot]]
            for r in range(clusters):
                picks = [inv_ref[r * slots + g * group + j] for j in range(group)]
                right = jnp.concatenate([right_v[k] for k in picks], axis=0)
                product = lax.dot_general(
                    qgroup[...], right, (((1,), (1,)), ((), ())),
                    preferred_element_type=jnp.float32,
                )
                coefficients = product[:columns]
                for j in range(1, group):
                    coefficients = jnp.where(
                        row_at == j, product[j * columns:(j + 1) * columns], coefficients
                    )
                left = jnp.concatenate([left_v[k] for k in picks], axis=0)
                out_ref[:, r * size:(r + 1) * size] += jnp.dot(
                    coefficients.astype(jnp.bfloat16), left, preferred_element_type=jnp.float32
                )
            return carry

        lax.fori_loop(0, slots // group, far_group, 0)

    for block, way, partner, valid in sent:
        def done(block=block, way=way, partner=partner):
            copy_of(block, way, partner).wait_send()
        done() if valid is None else pl.when(valid)(done)
    for index, off in enumerate(WINDOW):
        pl.when(reaches(off))(lambda index=index: feature_copy(index).wait_send())


def shards(
    charges, coords, requests, near_rows, near_src, local_pairs,
    far_rows, far_slots, far_left, far_right,
):
    columns, width = charges.shape
    pairs, rank, size = far_left.shape
    clusters = width // size
    n = requests.shape[1]
    slots = n * requests.shape[2]
    assert near_rows.shape[1] == clusters * 2 * clusters
    dense = pairs == clusters * slots and slots % (size // rank) == 0

    ids = jnp.arange(clusters, dtype=jnp.int32)
    first = (local_pairs[0, 0][:, None] == ids[None, :])
    second = (local_pairs[0, 1][:, None] == ids[None, :])
    mark = first[:, :, None] & second[:, None, :]
    mark = jnp.any(mark | mark.transpose(0, 2, 1), axis=0)
    mask = jnp.repeat(mark.astype(jnp.bfloat16), size, axis=1)

    code = far_rows[0] * slots + far_slots[0]
    if dense:
        order = jnp.arange(pairs, dtype=jnp.int32)
        inverse = jnp.sum(jnp.where(code[:, None] == order[None, :], order[:, None], 0), axis=0)
    else:
        inverse = code

    any_space = pl.BlockSpec(memory_space=pl.ANY)
    vmem = pl.BlockSpec(memory_space=pltpu.VMEM)
    smem = pl.BlockSpec(memory_space=pltpu.SMEM)
    held = far_left.shape if dense else (1, rank, size)
    half = jnp.bfloat16
    flops = 2 * width * width * 5 * (FEATURES + columns)
    potential = pl.pallas_call(
        functools.partial(body, n, dense),
        out_shape=jax.ShapeDtypeStruct((columns, width), jnp.float32),
        in_specs=[smem, smem, vmem, vmem, vmem, any_space, any_space],
        out_specs=vmem,
        scratch_shapes=[
            pltpu.VMEM((n, clusters, columns, size), half),
            pltpu.VMEM((FEATURES, width), half),
            pltpu.VMEM((4, FEATURES, width), half),
            pltpu.VMEM((width, FEATURES), half),
            pltpu.VMEM((FEATURES, width), half),
            pltpu.VMEM((columns * (size // rank), size), half),
            pltpu.VMEM(held, half),
            pltpu.VMEM(held, half),
            pltpu.SemaphoreType.DMA((4, n)),
            pltpu.SemaphoreType.DMA((n,)),
            pltpu.SemaphoreType.DMA((4,)),
            pltpu.SemaphoreType.DMA((4,)),
            pltpu.SemaphoreType.DMA((2,)),
        ],
        compiler_params=pltpu.CompilerParams(
            collective_id=0, has_side_effects=True, vmem_limit_bytes=56 * 1024 * 1024
        ),
        cost_estimate=pl.CostEstimate(
            flops=flops, bytes_accessed=2 * far_left.size * 2, transcendentals=5 * width * width
        ),
    )(inverse, requests.reshape(-1), charges, coords, mask, far_left, far_right)
    if dense:
        return potential

    blocks = charges.reshape(columns, clusters, size).transpose(1, 0, 2)
    every = lax.all_gather(blocks, "clu", axis=0, tiled=True)
    sources = jnp.arange(slots, dtype=jnp.int32) // requests.shape[2] * clusters
    fetched = every[sources + requests.reshape(-1)]

    def far_step(total, inputs):
        rows_here, slots_here, left_here, right_here = inputs
        coefficients = jnp.einsum(
            "pnb,pkb->pnk", fetched[slots_here], right_here, preferred_element_type=jnp.float32
        ).astype(half)
        term = jnp.einsum(
            "pnk,pka->pna", coefficients, left_here, preferred_element_type=jnp.float32
        )
        return (total.at[rows_here].add(term), None)

    far_inputs = (
        far_rows[0].reshape(-1, 64),
        far_slots[0].reshape(-1, 64),
        far_left.reshape(-1, 64, rank, size),
        far_right.reshape(-1, 64, rank, size),
    )
    total, _ = lax.scan(far_step, jnp.zeros((clusters, columns, size), jnp.float32), far_inputs)
    return potential + total.transpose(1, 0, 2).reshape(columns, width)


def solution(mesh):
    whole = ("groups", "clu")
    in_specs = (
        P(None, whole),
        P(None, whole),
        P(whole, None, None),
        P(whole, None),
        P(whole, None),
        P(whole, None, None),
        P(whole, None),
        P(whole, None),
        P(whole, None, None),
        P(whole, None, None),
    )
    return jax.shard_map(
        shards, mesh=mesh, in_specs=in_specs, out_specs=P(None, whole), check_vma=False
    )
```

```python
import functools

import jax
import jax.numpy as jnp
from jax import lax
from jax.experimental import pallas as pl
from jax.experimental.pallas import tpu as pltpu
from jax.sharding import PartitionSpec as P

kernel_scale = 1.0 / 64.0
softening = 0.04
MESH = pl.DeviceIdType.MESH
FEATURES = 16
WINDOW = (-2, -1, 1, 2)
PIECES = 1


def split3(values):
    high = values.astype(jnp.bfloat16)
    rest = values - high.astype(jnp.float32)
    mid = rest.astype(jnp.bfloat16)
    low = (rest - mid.astype(jnp.float32)).astype(jnp.bfloat16)
    return high.astype(jnp.float32), mid.astype(jnp.float32), low.astype(jnp.float32)


def point_features(coords):
    wide = coords.astype(jnp.float32)
    factor = 1.0 / (kernel_scale * kernel_scale)
    norm = (jnp.sum(wide * wide, axis=0, keepdims=True) + 0.5 * softening) * factor
    norms = jnp.concatenate(split3(norm), axis=0)
    ones = jnp.ones_like(norms)
    zeros = jnp.zeros((FEATURES - 9, wide.shape[1]), jnp.float32)
    source = jnp.concatenate([wide, norms, ones, zeros], axis=0)
    target = jnp.concatenate([wide * (-2.0 * factor), ones, norms, zeros], axis=0)
    return source, target


def body(
    n, dense,
    inv_ref, req_ref, q_ref, x_ref, mask_ref, left_hbm, right_hbm,
    out_ref,
    qbuf, fown, fbuf, ft, gown, qgroup, left_v, right_v,
    send_sem, recv_sem, fsend_sem, frecv_sem, load_sem,
):
    columns, width = q_ref.shape
    size = left_hbm.shape[2]
    rank = left_hbm.shape[1]
    clusters = width // size
    zs = n // 4
    me = lax.axis_index("clu")
    z = me // 4
    y = (me // 2) % 2
    core = me % 2
    sib = me + 1 - 2 * core
    other_y = me + 2 - 4 * y

    def block_id(z_at, y_at, core_at):
        return z_at * 4 + y_at * 2 + core_at

    barrier = pltpu.get_barrier_semaphore()
    partners = [(z > 0, me - 4), (z < zs - 1, me + 4), (None, other_y), (None, sib)]
    partners += [((me + off >= 0) & (me + off < n), me + off) for off in WINDOW]
    for valid, partner in partners:
        def greet(partner=partner):
            pl.semaphore_signal(barrier, inc=1, device_id={"clu": partner}, device_id_type=MESH)
        greet() if valid is None else pl.when(valid)(greet)

    if dense:
        load_left = pltpu.make_async_copy(left_hbm, left_v, load_sem.at[0])
        load_right = pltpu.make_async_copy(right_hbm, right_v, load_sem.at[1])
        load_right.start()
        load_left.start()
    source, target = point_features(x_ref[...])
    fown[...] = source.astype(jnp.bfloat16)
    gown[...] = target.astype(jnp.bfloat16)
    for c in range(clusters):
        qbuf[me, c] = q_ref[:, c * size:(c + 1) * size]

    pl.semaphore_wait(
        barrier, sum(1 if valid is None else valid.astype(jnp.int32) for valid, _ in partners)
    )

    sent = []

    def copies_of(block, way, partner):
        each = clusters // PIECES
        return [
            pltpu.make_async_remote_copy(
                src_ref=qbuf.at[block, pl.ds(piece * each, each)],
                dst_ref=qbuf.at[block, pl.ds(piece * each, each)],
                send_sem=send_sem.at[way, block, piece], recv_sem=recv_sem.at[block, piece],
                device_id={"clu": partner}, device_id_type=MESH,
            )
            for piece in range(PIECES)
        ]

    def send(block, way, partner, valid=None):
        def go():
            for copy in copies_of(block, way, partner):
                copy.start()
        go() if valid is None else pl.when(valid)(go)
        sent.append((block, way, partner, valid))

    def arrive(block, valid=None):
        def go():
            for copy in copies_of(block, 0, sib):
                copy.wait_recv()
        go() if valid is None else pl.when(valid)(go)

    def feature_copy(index):
        off = WINDOW[index]
        return pltpu.make_async_remote_copy(
            src_ref=fown, dst_ref=fbuf.at[index],
            send_sem=fsend_sem.at[index], recv_sem=frecv_sem.at[index],
            device_id={"clu": me + off}, device_id_type=MESH,
        )

    def reaches(off):
        return (me + off >= 0) & (me + off < n)

    for index in (1, 2, 0, 3):
        pl.when(reaches(WINDOW[index]))(lambda index=index: feature_copy(index).start())
    send(me, 3, sib)
    send(me, 2, other_y)
    send(me, 0, me + 4, z < zs - 1)
    send(me, 1, me - 4, z > 0)

    def boundary(k):
        if k <= zs - 1:
            for step, way, partner, more in ((-k, 0, me + 4, z < zs - 1), (k, 1, me - 4, z > 0)):
                there = (z + step >= 0) & (z + step < zs)
                block = block_id(z + step, y, core)
                arrive(block, there)
                send(block, way, partner, there & more)
                send(block, 2, other_y, there)
                send(block, 3, sib, there)
        if k <= zs:
            for step in ((0,) if k == 1 else (-(k - 1), k - 1)):
                there = None if step == 0 else (z + step >= 0) & (z + step < zs)
                block = block_id(z + step, 1 - y, core)
                arrive(block, there)
                send(block, 3, sib, there)
        if k == 1:
            arrive(sib)
        else:
            if k - 1 <= zs - 1:
                for step in (-(k - 1), k - 1):
                    arrive(block_id(z + step, y, 1 - core), (z + step >= 0) & (z + step < zs))
            for step in ((0,) if k == 2 else (-(k - 2), k - 2)):
                there = None if step == 0 else (z + step >= 0) & (z + step < zs)
                arrive(block_id(z + step, 1 - y, 1 - core), there)

    def product(charge, at):
        squared = jnp.dot(ft[at, :], gown[...], preferred_element_type=jnp.float32)
        blocks = lax.rsqrt(squared).astype(jnp.bfloat16)
        return jnp.dot(charge, blocks, preferred_element_type=jnp.float32)

    def set_features(values):
        ft[...] = values.astype(jnp.float32).T.astype(jnp.bfloat16)

    out_ref[...] = jnp.zeros_like(out_ref)

    set_features(fown[...])

    def local_step(e, carry):
        at = pl.ds(pl.multiple_of(e * size, size), size)
        out_ref[...] += product(qbuf[me, e], at) * mask_ref[pl.ds(e, 1), :]
        return carry

    lax.fori_loop(0, clusters, local_step, 0)

    def near(off):
        there = reaches(off)

        @pl.when(there)
        def _():
            for index, sent_off in enumerate(WINDOW):
                @pl.when(off == -sent_off)
                def _(index=index):
                    feature_copy(index).wait_recv()
                    set_features(fbuf[index])

            def near_step(e, carry):
                at = pl.ds(pl.multiple_of(e * size, size), size)
                out_ref[...] += product(qbuf[me + off, e], at)
                return carry

            lax.fori_loop(0, clusters, near_step, 0)

    place = me % 4

    def by_place(values):
        result = values[3]
        for index in (2, 1, 0):
            result = jnp.where(place == index, values[index], result)
        return result

    boundary(1)
    near(by_place((1, -1, 1, -1)))
    boundary(2)
    near(by_place((2, 1, -1, -2)))
    boundary(3)
    near(by_place((-1, 2, -2, 1)))
    boundary(4)
    near(by_place((-2, -2, 2, 2)))
    for k in range(5, zs + 3):
        boundary(k)

    if dense:
        load_right.wait()
        load_left.wait()
        slots_each = req_ref.shape[0] // n
        slots = n * slots_each
        group = size // rank
        row_at = lax.broadcasted_iota(jnp.int32, (columns, size), 1) // rank

        def far_group(g, carry):
            for j in range(group):
                slot = g * group + j
                qgroup[j * columns:(j + 1) * columns, :] = qbuf[slot // slots_each, req_ref[slot]]
            for r in range(clusters):
                picks = [inv_ref[r * slots + g * group + j] for j in range(group)]
                right = jnp.concatenate([right_v[k] for k in picks], axis=0)
                product = lax.dot_general(
                    qgroup[...], right, (((1,), (1,)), ((), ())),
                    preferred_element_type=jnp.float32,
                )
                coefficients = product[:columns]
                for j in range(1, group):
                    coefficients = jnp.where(
                        row_at == j, product[j * columns:(j + 1) * columns], coefficients
                    )
                left = jnp.concatenate([left_v[k] for k in picks], axis=0)
                out_ref[:, r * size:(r + 1) * size] += jnp.dot(
                    coefficients.astype(jnp.bfloat16), left, preferred_element_type=jnp.float32
                )
            return carry

        lax.fori_loop(0, slots // group, far_group, 0)

    for block, way, partner, valid in sent:
        def done(block=block, way=way, partner=partner):
            for copy in copies_of(block, way, partner):
                copy.wait_send()
        done() if valid is None else pl.when(valid)(done)
    for index, off in enumerate(WINDOW):
        pl.when(reaches(off))(lambda index=index: feature_copy(index).wait_send())


def shards(
    charges, coords, requests, near_rows, near_src, local_pairs,
    far_rows, far_slots, far_left, far_right,
):
    columns, width = charges.shape
    pairs, rank, size = far_left.shape
    clusters = width // size
    n = requests.shape[1]
    slots = n * requests.shape[2]
    assert near_rows.shape[1] == clusters * 2 * clusters
    dense = pairs == clusters * slots and slots % (size // rank) == 0

    ids = jnp.arange(clusters, dtype=jnp.int32)
    first = (local_pairs[0, 0][:, None] == ids[None, :])
    second = (local_pairs[0, 1][:, None] == ids[None, :])
    mark = first[:, :, None] & second[:, None, :]
    mark = jnp.any(mark | mark.transpose(0, 2, 1), axis=0)
    mask = jnp.repeat(mark.astype(jnp.float32), size, axis=1)

    code = far_rows[0] * slots + far_slots[0]
    if dense:
        order = jnp.arange(pairs, dtype=jnp.int32)
        inverse = jnp.max(jnp.where(code[:, None] == order[None, :], order[:, None], 0), axis=0)
    else:
        inverse = code

    any_space = pl.BlockSpec(memory_space=pl.ANY)
    vmem = pl.BlockSpec(memory_space=pltpu.VMEM)
    smem = pl.BlockSpec(memory_space=pltpu.SMEM)
    held = far_left.shape if dense else (1, rank, size)
    half = jnp.bfloat16
    flops = 2 * width * width * 5 * (FEATURES + columns)
    potential = pl.pallas_call(
        functools.partial(body, n, dense),
        out_shape=jax.ShapeDtypeStruct((columns, width), jnp.float32),
        in_specs=[smem, smem, vmem, vmem, vmem, any_space, any_space],
        out_specs=vmem,
        scratch_shapes=[
            pltpu.VMEM((n, clusters, columns, size), half),
            pltpu.VMEM((FEATURES, width), half),
            pltpu.VMEM((4, FEATURES, width), half),
            pltpu.VMEM((width, FEATURES), half),
            pltpu.VMEM((FEATURES, width), half),
            pltpu.VMEM((columns * (size // rank), size), half),
            pltpu.VMEM(held, half),
            pltpu.VMEM(held, half),
            pltpu.SemaphoreType.DMA((4, n, PIECES)),
            pltpu.SemaphoreType.DMA((n, PIECES)),
            pltpu.SemaphoreType.DMA((4,)),
            pltpu.SemaphoreType.DMA((4,)),
            pltpu.SemaphoreType.DMA((2,)),
        ],
        compiler_params=pltpu.CompilerParams(
            collective_id=0, has_side_effects=True, vmem_limit_bytes=56 * 1024 * 1024
        ),
        cost_estimate=pl.CostEstimate(
            flops=flops, bytes_accessed=2 * far_left.size * 2, transcendentals=5 * width * width
        ),
    )(inverse, requests.reshape(-1), charges, coords, mask, far_left, far_right)
    if dense:
        return potential

    blocks = charges.reshape(columns, clusters, size).transpose(1, 0, 2)
    every = lax.all_gather(blocks, "clu", axis=0, tiled=True)
    sources = jnp.arange(slots, dtype=jnp.int32) // requests.shape[2] * clusters
    fetched = every[sources + requests.reshape(-1)]

    def far_step(total, inputs):
        rows_here, slots_here, left_here, right_here = inputs
        coefficients = jnp.einsum(
            "pnb,pkb->pnk", fetched[slots_here], right_here, preferred_element_type=jnp.float32
        ).astype(half)
        term = jnp.einsum(
            "pnk,pka->pna", coefficients, left_here, preferred_element_type=jnp.float32
        )
        return (total.at[rows_here].add(term), None)

    far_inputs = (
        far_rows[0].reshape(-1, 64),
        far_slots[0].reshape(-1, 64),
        far_left.reshape(-1, 64, rank, size),
        far_right.reshape(-1, 64, rank, size),
    )
    total, _ = lax.scan(far_step, jnp.zeros((clusters, columns, size), jnp.float32), far_inputs)
    return potential + total.transpose(1, 0, 2).reshape(columns, width)


def solution(mesh):
    whole = ("groups", "clu")
    in_specs = (
        P(None, whole),
        P(None, whole),
        P(whole, None, None),
        P(whole, None),
        P(whole, None),
        P(whole, None, None),
        P(whole, None),
        P(whole, None),
        P(whole, None, None),
        P(whole, None, None),
    )
    return jax.shard_map(
        shards, mesh=mesh, in_specs=in_specs, out_specs=P(None, whole), check_vma=False
    )
```

```python
import functools

import jax
import jax.numpy as jnp
from jax import lax
from jax.experimental import pallas as pl
from jax.experimental.pallas import tpu as pltpu
from jax.sharding import PartitionSpec as P

kernel_scale = 1.0 / 64.0
softening = 0.04
MESH = pl.DeviceIdType.MESH
FEATURES = 16
WINDOW = (-2, -1, 1, 2)
PIECES = 1
TOGETHER = 4


def split3(values):
    high = values.astype(jnp.bfloat16)
    rest = values - high.astype(jnp.float32)
    mid = rest.astype(jnp.bfloat16)
    low = (rest - mid.astype(jnp.float32)).astype(jnp.bfloat16)
    return high.astype(jnp.float32), mid.astype(jnp.float32), low.astype(jnp.float32)


def point_features(coords):
    wide = coords.astype(jnp.float32)
    factor = 1.0 / (kernel_scale * kernel_scale)
    norm = (jnp.sum(wide * wide, axis=0, keepdims=True) + 0.5 * softening) * factor
    norms = jnp.concatenate(split3(norm), axis=0)
    ones = jnp.ones_like(norms)
    zeros = jnp.zeros((FEATURES - 9, wide.shape[1]), jnp.float32)
    source = jnp.concatenate([wide, norms, ones, zeros], axis=0)
    target = jnp.concatenate([wide * (-2.0 * factor), ones, norms, zeros], axis=0)
    return source, target


def body(
    n, dense,
    req_ref, pairs_ref, rows_ref, slots_ref, q_ref, x_ref, left_hbm, right_hbm,
    out_ref,
    qbuf, fown, fbuf, ft, gown, mask_ref, left_v, right_v, inv_v, inv_ref,
    send_sem, recv_sem, fsend_sem, frecv_sem, load_sem,
):
    columns, width = q_ref.shape
    size = left_hbm.shape[2]
    rank = left_hbm.shape[1]
    clusters = width // size
    zs = n // 4
    me = lax.axis_index("clu")
    z = me // 4
    y = (me // 2) % 2
    core = me % 2
    sib = me + 1 - 2 * core
    other_y = me + 2 - 4 * y

    def block_id(z_at, y_at, core_at):
        return z_at * 4 + y_at * 2 + core_at

    barrier = pltpu.get_barrier_semaphore()
    partners = [(z > 0, me - 4), (z < zs - 1, me + 4), (None, other_y), (None, sib)]
    partners += [((me + off >= 0) & (me + off < n), me + off) for off in WINDOW]
    for valid, partner in partners:
        def greet(partner=partner):
            pl.semaphore_signal(barrier, inc=1, device_id={"clu": partner}, device_id_type=MESH)
        greet() if valid is None else pl.when(valid)(greet)

    if dense:
        load_left = pltpu.make_async_copy(left_hbm, left_v, load_sem.at[0])
        load_right = pltpu.make_async_copy(right_hbm, right_v, load_sem.at[1])
        load_right.start()
        load_left.start()
    for c in range(clusters):
        qbuf[me, c] = q_ref[:, c * size:(c + 1) * size]

    pl.semaphore_wait(
        barrier, sum(1 if valid is None else valid.astype(jnp.int32) for valid, _ in partners)
    )

    sent = []

    def copies_of(block, way, partner):
        each = clusters // PIECES
        return [
            pltpu.make_async_remote_copy(
                src_ref=qbuf.at[block, pl.ds(piece * each, each)],
                dst_ref=qbuf.at[block, pl.ds(piece * each, each)],
                send_sem=send_sem.at[way, block, piece], recv_sem=recv_sem.at[block, piece],
                device_id={"clu": partner}, device_id_type=MESH,
            )
            for piece in range(PIECES)
        ]

    def send(block, way, partner, valid=None):
        def go():
            for copy in copies_of(block, way, partner):
                copy.start()
        go() if valid is None else pl.when(valid)(go)
        sent.append((block, way, partner, valid))

    def arrive(block, valid=None):
        def go():
            for copy in copies_of(block, 0, sib):
                copy.wait_recv()
        go() if valid is None else pl.when(valid)(go)

    def feature_copy(index):
        off = WINDOW[index]
        return pltpu.make_async_remote_copy(
            src_ref=fown, dst_ref=fbuf.at[index],
            send_sem=fsend_sem.at[index], recv_sem=frecv_sem.at[index],
            device_id={"clu": me + off}, device_id_type=MESH,
        )

    def reaches(off):
        return (me + off >= 0) & (me + off < n)

    send(me, 0, me + 4, z < zs - 1)
    send(me, 1, me - 4, z > 0)
    send(me, 2, other_y)
    send(me, 3, sib)
    source, target = point_features(x_ref[...])
    fown[...] = source.astype(jnp.bfloat16)
    gown[...] = target.astype(jnp.bfloat16)
    for index in (1, 2, 0, 3):
        pl.when(reaches(WINDOW[index]))(lambda index=index: feature_copy(index).start())

    def on_z(step):
        return None if step == 0 else (z + step >= 0) & (z + step < zs)

    def both_ways(k):
        return (0,) if k == 0 else (-k, k)

    def along_z(k):
        if 1 <= k < zs:
            for step, way, partner, more in ((-k, 0, me + 4, z < zs - 1), (k, 1, me - 4, z > 0)):
                block = block_id(z + step, y, core)
                arrive(block, on_z(step))
                send(block, way, partner, on_z(step) & more)
                send(block, 2, other_y, on_z(step))
                send(block, 3, sib, on_z(step))

    def across_y(k):
        if 0 <= k < zs:
            for step in both_ways(k):
                block = block_id(z + step, 1 - y, core)
                arrive(block, on_z(step))
                send(block, 3, sib, on_z(step))

    def from_sibling(k, y_at):
        if 0 <= k < zs:
            for step in both_ways(k):
                arrive(block_id(z + step, y_at, 1 - core), on_z(step))

    def product(block, first, count):
        at = pl.ds(pl.multiple_of(first * size, size), count * size)
        squared = jnp.dot(ft[at, :], gown[...], preferred_element_type=jnp.float32)
        blocks = lax.rsqrt(squared).astype(jnp.bfloat16)
        charge = jnp.concatenate([qbuf[block, first + i] for i in range(count)], axis=1)
        return jnp.dot(charge, blocks, preferred_element_type=jnp.float32)

    def set_features(values):
        ft[...] = values.astype(jnp.float32).T.astype(jnp.bfloat16)

    out_ref[...] = jnp.zeros_like(out_ref)

    set_features(fown[...])
    entry = lax.broadcasted_iota(jnp.int32, (clusters, width), 0) * clusters
    entry = entry + lax.broadcasted_iota(jnp.int32, (clusters, width), 1) // size
    mark = entry < 0
    for k in range(pairs_ref.shape[2]):
        first, second = pairs_ref[0, 0, k], pairs_ref[0, 1, k]
        mark = mark | (entry == first * clusters + second) | (entry == second * clusters + first)
    mask_ref[...] = mark.astype(jnp.float32)

    if dense:
        slots = n * req_ref.shape[2]
        pairs = clusters * slots
        code = jnp.broadcast_to(rows_ref[...] * slots + slots_ref[...], (8, pairs)).T[:, :1]
        found = code == lax.broadcasted_iota(jnp.int32, (pairs, pairs), 1)
        number = lax.broadcasted_iota(jnp.int32, (pairs, pairs), 0)
        table = jnp.max(jnp.where(found, number, 0), axis=0, keepdims=True)
        inv_v[...] = jnp.broadcast_to(table, (8, pairs))
        to_scalars = pltpu.make_async_copy(inv_v, inv_ref, load_sem.at[2])
        to_scalars.start()

    def local_step(e, carry):
        out_ref[...] += product(me, e, 1) * mask_ref[pl.ds(e, 1), :]
        return carry

    lax.fori_loop(0, clusters, local_step, 0, unroll=2)

    def near(off):
        there = reaches(off)

        @pl.when(there)
        def _():
            for index, sent_off in enumerate(WINDOW):
                @pl.when(off == -sent_off)
                def _(index=index):
                    feature_copy(index).wait_recv()
                    set_features(fbuf[index])

            def near_step(step, carry):
                out_ref[...] += product(me + off, step * TOGETHER, TOGETHER)
                return carry

            lax.fori_loop(0, clusters // TOGETHER, near_step, 0)

    place = me % 4

    def by_place(values):
        result = values[3]
        for index in (2, 1, 0):
            result = jnp.where(place == index, values[index], result)
        return result

    along_z(1)
    from_sibling(0, y)
    near(by_place((1, -1, 1, -1)))
    along_z(2)
    across_y(0)
    from_sibling(1, y)
    from_sibling(0, 1 - y)
    near(by_place((2, 1, -1, -2)))
    along_z(3)
    across_y(1)
    from_sibling(2, y)
    from_sibling(1, 1 - y)
    near(by_place((-1, 2, -2, 1)))
    across_y(2)
    from_sibling(3, y)
    near(by_place((-2, -2, 2, 2)))
    across_y(3)
    from_sibling(2, 1 - y)
    from_sibling(3, 1 - y)
    for k in range(4, zs):
        along_z(k)
        across_y(k)
        from_sibling(k, y)
        from_sibling(k, 1 - y)

    if dense:
        load_right.wait()
        load_left.wait()
        to_scalars.wait()
        slots_each = req_ref.shape[2]
        group = size // rank

        def far_group(g, carry):
            def pick(r, j):
                return inv_ref[0, r * slots + g * group + j]

            parts = []
            for j in range(group):
                slot = g * group + j
                owner = slot // slots_each
                charge = qbuf[owner, req_ref[0, owner, slot % slots_each]]
                right = jnp.concatenate([right_v[pick(r, j)] for r in range(clusters)], axis=0)
                parts.append(lax.dot_general(
                    right, charge, (((1,), (1,)), ((), ())), preferred_element_type=jnp.float32
                ))
            for r in range(clusters):
                turned = jnp.concatenate(
                    [part[r * rank:(r + 1) * rank] for part in parts], axis=0
                )
                left = jnp.concatenate([left_v[pick(r, j)] for j in range(group)], axis=0)
                out_ref[:, r * size:(r + 1) * size] += jnp.dot(
                    turned.T.astype(jnp.bfloat16), left, preferred_element_type=jnp.float32
                )
            return carry

        lax.fori_loop(0, slots // group, far_group, 0)

    for block, way, partner, valid in sent:
        def done(block=block, way=way, partner=partner):
            for copy in copies_of(block, way, partner):
                copy.wait_send()
        done() if valid is None else pl.when(valid)(done)
    for index, off in enumerate(WINDOW):
        pl.when(reaches(off))(lambda index=index: feature_copy(index).wait_send())


def shards(
    charges, coords, requests, near_rows, near_src, local_pairs,
    far_rows, far_slots, far_left, far_right,
):
    columns, width = charges.shape
    pairs, rank, size = far_left.shape
    clusters = width // size
    n = requests.shape[1]
    slots = n * requests.shape[2]
    assert near_rows.shape[1] == clusters * 2 * clusters
    dense = pairs == clusters * slots and slots % (size // rank) == 0

    any_space = pl.BlockSpec(memory_space=pl.ANY)
    vmem = pl.BlockSpec(memory_space=pltpu.VMEM)
    smem = pl.BlockSpec(memory_space=pltpu.SMEM)
    held = far_left.shape if dense else (1, rank, size)
    half = jnp.bfloat16
    flops = 2 * width * width * 5 * (FEATURES + columns)
    potential = pl.pallas_call(
        functools.partial(body, n, dense),
        out_shape=jax.ShapeDtypeStruct((columns, width), jnp.float32),
        in_specs=[smem, smem, vmem, vmem, vmem, vmem, any_space, any_space],
        out_specs=vmem,
        scratch_shapes=[
            pltpu.VMEM((n, clusters, columns, size), half),
            pltpu.VMEM((FEATURES, width), half),
            pltpu.VMEM((4, FEATURES, width), half),
            pltpu.VMEM((width, FEATURES), half),
            pltpu.VMEM((FEATURES, width), half),
            pltpu.VMEM((clusters, width), jnp.float32),
            pltpu.VMEM(held, half),
            pltpu.VMEM(held, half),
            pltpu.VMEM((8, pairs), jnp.int32),
            pltpu.SMEM((8, pairs), jnp.int32),
            pltpu.SemaphoreType.DMA((4, n, PIECES)),
            pltpu.SemaphoreType.DMA((n, PIECES)),
            pltpu.SemaphoreType.DMA((4,)),
            pltpu.SemaphoreType.DMA((4,)),
            pltpu.SemaphoreType.DMA((3,)),
        ],
        compiler_params=pltpu.CompilerParams(
            collective_id=0, has_side_effects=True, vmem_limit_bytes=56 * 1024 * 1024
        ),
        cost_estimate=pl.CostEstimate(
            flops=flops, bytes_accessed=2 * far_left.size * 2, transcendentals=5 * width * width
        ),
    )(requests, local_pairs, far_rows, far_slots, charges, coords, far_left, far_right)
    if dense:
        return potential

    blocks = charges.reshape(columns, clusters, size).transpose(1, 0, 2)
    every = lax.all_gather(blocks, "clu", axis=0, tiled=True)
    sources = jnp.arange(slots, dtype=jnp.int32) // requests.shape[2] * clusters
    fetched = every[sources + requests.reshape(-1)]

    def far_step(total, inputs):
        rows_here, slots_here, left_here, right_here = inputs
        coefficients = jnp.einsum(
            "pnb,pkb->pnk", fetched[slots_here], right_here, preferred_element_type=jnp.float32
        ).astype(half)
        term = jnp.einsum(
            "pnk,pka->pna", coefficients, left_here, preferred_element_type=jnp.float32
        )
        return (total.at[rows_here].add(term), None)

    far_inputs = (
        far_rows[0].reshape(-1, 64),
        far_slots[0].reshape(-1, 64),
        far_left.reshape(-1, 64, rank, size),
        far_right.reshape(-1, 64, rank, size),
    )
    total, _ = lax.scan(far_step, jnp.zeros((clusters, columns, size), jnp.float32), far_inputs)
    return potential + total.transpose(1, 0, 2).reshape(columns, width)


def solution(mesh):
    whole = ("groups", "clu")
    in_specs = (
        P(None, whole),
        P(None, whole),
        P(whole, None, None),
        P(whole, None),
        P(whole, None),
        P(whole, None, None),
        P(whole, None),
        P(whole, None),
        P(whole, None, None),
        P(whole, None, None),
    )
    return jax.shard_map(
        shards, mesh=mesh, in_specs=in_specs, out_specs=P(None, whole), check_vma=False
    )
```

```python
import functools

import jax
import jax.numpy as jnp
from jax import lax
from jax.experimental import pallas as pl
from jax.experimental.pallas import tpu as pltpu
from jax.sharding import PartitionSpec as P

kernel_scale = 1.0 / 64.0
softening = 0.04
MESH = pl.DeviceIdType.MESH
FEATURES = 16
WINDOW = (-2, -1, 1, 2)
PIECES = 1
TOGETHER = 4


def split3(values):
    high = values.astype(jnp.bfloat16)
    rest = values - high.astype(jnp.float32)
    mid = rest.astype(jnp.bfloat16)
    low = (rest - mid.astype(jnp.float32)).astype(jnp.bfloat16)
    return high.astype(jnp.float32), mid.astype(jnp.float32), low.astype(jnp.float32)


def point_features(coords):
    wide = coords.astype(jnp.float32)
    factor = 1.0 / (kernel_scale * kernel_scale)
    norm = (jnp.sum(wide * wide, axis=0, keepdims=True) + 0.5 * softening) * factor
    norms = jnp.concatenate(split3(norm), axis=0)
    ones = jnp.ones_like(norms)
    zeros = jnp.zeros((FEATURES - 9, wide.shape[1]), jnp.float32)
    source = jnp.concatenate([wide, norms, ones, zeros], axis=0)
    target = jnp.concatenate([wide * (-2.0 * factor), ones, norms, zeros], axis=0)
    return source, target


def body(
    n, dense,
    req_ref, pairs_ref, rows_ref, slots_ref, q_ref, x_ref, left_hbm, right_hbm,
    out_ref,
    qbuf, fown, fbuf, ft, gown, mask_ref, left_v, right_v, inv_v, inv_ref,
    send_sem, recv_sem, fsend_sem, frecv_sem, load_sem,
):
    columns, width = q_ref.shape
    size = left_hbm.shape[2]
    rank = left_hbm.shape[1]
    clusters = width // size
    zs = n // 4
    me = lax.axis_index("clu")
    z = me // 4
    y = (me // 2) % 2
    core = me % 2
    sib = me + 1 - 2 * core
    other_y = me + 2 - 4 * y

    def block_id(z_at, y_at, core_at):
        return z_at * 4 + y_at * 2 + core_at

    barrier = pltpu.get_barrier_semaphore()
    partners = [(z > 0, me - 4), (z < zs - 1, me + 4), (None, other_y), (None, sib)]
    partners += [((me + off >= 0) & (me + off < n), me + off) for off in WINDOW]
    for valid, partner in partners:
        def greet(partner=partner):
            pl.semaphore_signal(barrier, inc=1, device_id={"clu": partner}, device_id_type=MESH)
        greet() if valid is None else pl.when(valid)(greet)

    if dense:
        load_left = pltpu.make_async_copy(left_hbm, left_v, load_sem.at[0])
        load_right = pltpu.make_async_copy(right_hbm, right_v, load_sem.at[1])
        load_right.start()
        load_left.start()
    for c in range(clusters):
        qbuf[me, c] = q_ref[:, c * size:(c + 1) * size]

    pl.semaphore_wait(
        barrier, sum(1 if valid is None else valid.astype(jnp.int32) for valid, _ in partners)
    )

    sent = []

    def copies_of(block, way, partner):
        each = clusters // PIECES
        return [
            pltpu.make_async_remote_copy(
                src_ref=qbuf.at[block, pl.ds(piece * each, each)],
                dst_ref=qbuf.at[block, pl.ds(piece * each, each)],
                send_sem=send_sem.at[way, block, piece], recv_sem=recv_sem.at[block, piece],
                device_id={"clu": partner}, device_id_type=MESH,
            )
            for piece in range(PIECES)
        ]

    def send(block, way, partner, valid=None):
        def go():
            for copy in copies_of(block, way, partner):
                copy.start()
        go() if valid is None else pl.when(valid)(go)
        sent.append((block, way, partner, valid))

    def arrive(block, valid=None):
        def go():
            for copy in copies_of(block, 0, sib):
                copy.wait_recv()
        go() if valid is None else pl.when(valid)(go)

    def feature_copy(index):
        off = WINDOW[index]
        return pltpu.make_async_remote_copy(
            src_ref=fown, dst_ref=fbuf.at[index],
            send_sem=fsend_sem.at[index], recv_sem=frecv_sem.at[index],
            device_id={"clu": me + off}, device_id_type=MESH,
        )

    def reaches(off):
        return (me + off >= 0) & (me + off < n)

    send(me, 0, me + 4, z < zs - 1)
    send(me, 1, me - 4, z > 0)
    send(me, 2, other_y)
    send(me, 3, sib)
    source, target = point_features(x_ref[...])
    fown[...] = source.astype(jnp.bfloat16)
    gown[...] = target.astype(jnp.bfloat16)
    for index in (1, 2, 0, 3):
        pl.when(reaches(WINDOW[index]))(lambda index=index: feature_copy(index).start())

    def on_z(step):
        return None if step == 0 else (z + step >= 0) & (z + step < zs)

    def both_ways(k):
        return (0,) if k == 0 else (-k, k)

    def along_z(k):
        if 1 <= k < zs:
            for step, way, partner, more in ((-k, 0, me + 4, z < zs - 1), (k, 1, me - 4, z > 0)):
                block = block_id(z + step, y, core)
                arrive(block, on_z(step))
                send(block, way, partner, on_z(step) & more)
                send(block, 2, other_y, on_z(step))
                send(block, 3, sib, on_z(step))

    def across_y(k):
        if 0 <= k < zs:
            for step in both_ways(k):
                block = block_id(z + step, 1 - y, core)
                arrive(block, on_z(step))
                send(block, 3, sib, on_z(step))

    def from_sibling(k, y_at):
        if 0 <= k < zs:
            for step in both_ways(k):
                arrive(block_id(z + step, y_at, 1 - core), on_z(step))

    def product(block, first, count):
        at = pl.ds(pl.multiple_of(first * size, size), count * size)
        squared = jnp.dot(ft[at, :], gown[...], preferred_element_type=jnp.float32)
        blocks = lax.rsqrt(squared).astype(jnp.bfloat16)
        charge = jnp.concatenate([qbuf[block, first + i] for i in range(count)], axis=1)
        return jnp.dot(charge, blocks, preferred_element_type=jnp.float32)

    def set_features(values):
        ft[...] = values.astype(jnp.float32).T.astype(jnp.bfloat16)

    out_ref[...] = jnp.zeros_like(out_ref)

    set_features(fown[...])
    entry = lax.broadcasted_iota(jnp.int32, (clusters, width), 0) * clusters
    entry = entry + lax.broadcasted_iota(jnp.int32, (clusters, width), 1) // size
    mark = entry < 0
    for k in range(pairs_ref.shape[2]):
        first, second = pairs_ref[0, 0, k], pairs_ref[0, 1, k]
        mark = mark | (entry == first * clusters + second) | (entry == second * clusters + first)
    mask_ref[...] = mark.astype(jnp.float32)

    if dense:
        slots = n * req_ref.shape[2]
        pairs = clusters * slots
        code = jnp.broadcast_to(rows_ref[...] * slots + slots_ref[...], (8, pairs)).T[:, :1]
        found = code == lax.broadcasted_iota(jnp.int32, (pairs, pairs), 1)
        number = lax.broadcasted_iota(jnp.int32, (pairs, pairs), 0)
        table = jnp.max(jnp.where(found, number, 0), axis=0, keepdims=True)
        inv_v[...] = jnp.broadcast_to(table, (8, pairs))
        to_scalars = pltpu.make_async_copy(inv_v, inv_ref, load_sem.at[2])
        to_scalars.start()

    def local_step(e, carry):
        out_ref[...] += product(me, e, 1) * mask_ref[pl.ds(e, 1), :]
        return carry

    lax.fori_loop(0, clusters, local_step, 0, unroll=2)

    def near_start(off):
        @pl.when(reaches(off))
        def _():
            for index, sent_off in enumerate(WINDOW):
                @pl.when(off == -sent_off)
                def _(index=index):
                    feature_copy(index).wait_recv()
                    set_features(fbuf[index])

    def near_part(off, first, last):
        @pl.when(reaches(off))
        def _():
            def near_step(step, carry):
                out_ref[...] += product(me + off, step * TOGETHER, TOGETHER)
                return carry

            lax.fori_loop(first, last, near_step, 0)

    place = me % 4

    def by_place(values):
        result = values[3]
        for index in (2, 1, 0):
            result = jnp.where(place == index, values[index], result)
        return result

    steps = clusters // TOGETHER
    along_z(1)
    from_sibling(0, y)
    off = by_place((1, -1, 1, -1))
    near_start(off)
    near_part(off, 0, steps // 2)
    along_z(2)
    across_y(0)
    near_part(off, steps // 2, steps)
    from_sibling(1, y)
    from_sibling(0, 1 - y)
    off = by_place((2, 1, -1, -2))
    near_start(off)
    near_part(off, 0, steps // 2)
    along_z(3)
    across_y(1)
    near_part(off, steps // 2, steps)
    from_sibling(2, y)
    from_sibling(1, 1 - y)
    off = by_place((-1, 2, -2, 1))
    near_start(off)
    near_part(off, 0, steps)
    across_y(2)
    from_sibling(3, y)
    off = by_place((-2, -2, 2, 2))
    near_start(off)
    near_part(off, 0, steps)
    from_sibling(2, 1 - y)

    def last_arrivals():
        across_y(3)
        from_sibling(3, 1 - y)
        for k in range(4, zs):
            along_z(k)
            across_y(k)
            from_sibling(k, y)
            from_sibling(k, 1 - y)

    if not dense:
        last_arrivals()
    else:
        load_right.wait()
        load_left.wait()
        to_scalars.wait()
        slots_each = req_ref.shape[2]
        group = size // rank

        def far_group(g, carry):
            def pick(r, j):
                return inv_ref[0, r * slots + g * group + j]

            parts = []
            for j in range(group):
                slot = g * group + j
                owner = slot // slots_each
                wanted = req_ref[0, owner, slot % slots_each]
                charge = qbuf[owner, 0]
                for c in range(1, clusters):
                    charge = jnp.where(wanted == c, qbuf[owner, c], charge)
                right = jnp.concatenate([right_v[pick(r, j)] for r in range(clusters)], axis=0)
                parts.append(lax.dot_general(
                    right, charge, (((1,), (1,)), ((), ())), preferred_element_type=jnp.float32
                ))
            for r in range(clusters):
                turned = jnp.concatenate(
                    [part[r * rank:(r + 1) * rank] for part in parts], axis=0
                )
                left = jnp.concatenate([left_v[pick(r, j)] for j in range(group)], axis=0)
                out_ref[:, r * size:(r + 1) * size] += jnp.dot(
                    turned.T.astype(jnp.bfloat16), left, preferred_element_type=jnp.float32
                )
            return carry

        above = (2 * z < zs).astype(jnp.int32)
        lax.fori_loop(1 - above, zs - above, far_group, 0)
        last_arrivals()
        far_group(above * (zs - 1), 0)

    for block, way, partner, valid in sent:
        def done(block=block, way=way, partner=partner):
            for copy in copies_of(block, way, partner):
                copy.wait_send()
        done() if valid is None else pl.when(valid)(done)
    for index, off in enumerate(WINDOW):
        pl.when(reaches(off))(lambda index=index: feature_copy(index).wait_send())


def shards(
    charges, coords, requests, near_rows, near_src, local_pairs,
    far_rows, far_slots, far_left, far_right,
):
    columns, width = charges.shape
    pairs, rank, size = far_left.shape
    clusters = width // size
    n = requests.shape[1]
    slots = n * requests.shape[2]
    assert near_rows.shape[1] == clusters * 2 * clusters
    dense = pairs == clusters * slots and size // rank == 4 * requests.shape[2] and n <= 16

    any_space = pl.BlockSpec(memory_space=pl.ANY)
    vmem = pl.BlockSpec(memory_space=pltpu.VMEM)
    smem = pl.BlockSpec(memory_space=pltpu.SMEM)
    held = far_left.shape if dense else (1, rank, size)
    half = jnp.bfloat16
    flops = 2 * width * width * 5 * (FEATURES + columns)
    potential = pl.pallas_call(
        functools.partial(body, n, dense),
        out_shape=jax.ShapeDtypeStruct((columns, width), jnp.float32),
        in_specs=[smem, smem, vmem, vmem, vmem, vmem, any_space, any_space],
        out_specs=vmem,
        scratch_shapes=[
            pltpu.VMEM((n, clusters, columns, size), half),
            pltpu.VMEM((FEATURES, width), half),
            pltpu.VMEM((4, FEATURES, width), half),
            pltpu.VMEM((width, FEATURES), half),
            pltpu.VMEM((FEATURES, width), half),
            pltpu.VMEM((clusters, width), jnp.float32),
            pltpu.VMEM(held, half),
            pltpu.VMEM(held, half),
            pltpu.VMEM((8, pairs), jnp.int32),
            pltpu.SMEM((8, pairs), jnp.int32),
            pltpu.SemaphoreType.DMA((4, n, PIECES)),
            pltpu.SemaphoreType.DMA((n, PIECES)),
            pltpu.SemaphoreType.DMA((4,)),
            pltpu.SemaphoreType.DMA((4,)),
            pltpu.SemaphoreType.DMA((3,)),
        ],
        compiler_params=pltpu.CompilerParams(
            collective_id=0, has_side_effects=True, vmem_limit_bytes=56 * 1024 * 1024
        ),
        cost_estimate=pl.CostEstimate(
            flops=flops, bytes_accessed=2 * far_left.size * 2, transcendentals=5 * width * width
        ),
    )(requests, local_pairs, far_rows, far_slots, charges, coords, far_left, far_right)
    if dense:
        return potential

    blocks = charges.reshape(columns, clusters, size).transpose(1, 0, 2)
    every = lax.all_gather(blocks, "clu", axis=0, tiled=True)
    sources = jnp.arange(slots, dtype=jnp.int32) // requests.shape[2] * clusters
    fetched = every[sources + requests.reshape(-1)]

    def far_step(total, inputs):
        rows_here, slots_here, left_here, right_here = inputs
        coefficients = jnp.einsum(
            "pnb,pkb->pnk", fetched[slots_here], right_here, preferred_element_type=jnp.float32
        ).astype(half)
        term = jnp.einsum(
            "pnk,pka->pna", coefficients, left_here, preferred_element_type=jnp.float32
        )
        return (total.at[rows_here].add(term), None)

    far_inputs = (
        far_rows[0].reshape(-1, 64),
        far_slots[0].reshape(-1, 64),
        far_left.reshape(-1, 64, rank, size),
        far_right.reshape(-1, 64, rank, size),
    )
    total, _ = lax.scan(far_step, jnp.zeros((clusters, columns, size), jnp.float32), far_inputs)
    return potential + total.transpose(1, 0, 2).reshape(columns, width)


def solution(mesh):
    whole = ("groups", "clu")
    in_specs = (
        P(None, whole),
        P(None, whole),
        P(whole, None, None),
        P(whole, None),
        P(whole, None),
        P(whole, None, None),
        P(whole, None),
        P(whole, None),
        P(whole, None, None),
        P(whole, None, None),
    )
    return jax.shard_map(
        shards, mesh=mesh, in_specs=in_specs, out_specs=P(None, whole), check_vma=False
    )
```
